32 devices in a mesh: groups: 2 (over x), hid: 16 (over z, y, core).
Axes of the slice: x: 2, y: 2, z: 4, core: 2. Of those that a mesh axis runs over, the one named last changes fastest.
Arguments:
- tokens: bfloat16 [2, 32, 8192], P(None, ('groups', 'hid')), parts along dimension 1, may hold values from -6 to 6
- positions: int32 [32], P(('groups', 'hid')), parts along dimension 0, may hold values from 0 to 8191
- lengths: int32 [32], P(('groups', 'hid')), parts along dimension 0, may hold values from 64 to 510, as said below
- w_query: bfloat16 [8192, 8192], P(None, 'hid'), may hold values from -0.0625 to 0.0625
- w_key: bfloat16 [8192, 1024], P(None, 'hid'), may hold values from -0.0625 to 0.0625
- w_value: bfloat16 [8192, 1024], P(None, 'hid'), may hold values from -0.0625 to 0.0625
- w_out: bfloat16 [8192, 8192], P('hid'), may hold values from -1.5 to 1.5
- cache_keys: bfloat16 [32, 512, 1024], P(('groups', 'hid')), parts along dimension 0, may hold values from -128 to 128
- cache_values: bfloat16 [32, 512, 1024], P(('groups', 'hid')), parts along dimension 0, may hold values from -4 to 4
Outputs:
- attended: bfloat16 [2, 32, 8192], P(None, ('groups', 'hid')), parts along dimension 1
The draws below stay inside these ranges and needn't reach their ends.
There are 2 independent parts, one for each index of `groups`. The reference program is written for one: setup_inputs(seed, part) draws one part's arguments, and reference() takes and returns one part's arrays. A program takes and returns all parts, laid end to end along the dimension named above; an argument that names none is the same for every part. Nothing has to cross between parts.
Inputs may be any that keep to these rules, and one draw needn't show every extreme that they name: Row r's cache holds valid keys and values at positions 0 to lengths[r] - 1; some row has length 510.
All inputs are finite; a program needn't handle non-finite values.
Results may differ from the reference program's by a relative error of at most 0.012.
Values may be sent and summed in bfloat16 or wider, within the bound.
A program may use at most 128 MiB of HBM per device.

```python
import math
import jax
import jax.numpy as jnp
from jax import lax

D = 8192
HEADS = 64
KV_HEADS = 8
HEAD = 128
CACHE = 512
BATCH = 16


def draw_lengths(key, part):
    key = jax.random.fold_in(key, 5)
    first_key, second_key = jax.random.split(key)
    filled = jax.random.randint(first_key, (BATCH,), CACHE // 8, CACHE - 1)
    longest = jax.random.randint(second_key, (), 0, BATCH)
    return filled.at[longest].set(CACHE - 2)


def draw_cache_keys(key, part):
    key = jax.random.fold_in(key, 11)
    base_key = jax.random.fold_in(key, 0)
    shape = (BATCH, CACHE, KV_HEADS * HEAD)
    return jnp.clip(jax.random.normal(base_key, shape, jnp.float32), -4.0, 4.0).astype(jnp.bfloat16)


def touch_ends(drawn, stream_key, smallest, largest):
    dims = drawn.shape
    place = [jax.random.randint(jax.random.fold_in(stream_key, axis), (), 0, dims[axis]) for axis in range(len(dims))]
    drawn = drawn.at[tuple(place)].set(smallest)
    longest = dims.index(max(dims))
    place[longest] = (place[longest] + 1) % dims[longest]
    return drawn.at[tuple(place)].set(largest)


def shard_levels(key, extent, cuts, smallest, largest):
    gain, own = 1.0, jax.random.fold_in(key, 6)
    for position, shards_of in cuts:
        draws = jnp.exp(jax.random.uniform(jax.random.fold_in(own, position), (shards_of,), jnp.float32, smallest / len(cuts), largest / len(cuts)))
        gain = gain * jnp.repeat(draws, extent[position] // shards_of).reshape([-1 if axis == position else 1 for axis in range(len(extent))])
    return gain


def bell_draw(rng, dims, scale, bound, cuts=(), held_as=jnp.bfloat16):
    loudness = shard_levels(rng, dims, cuts, -0.22, 0.18) if cuts else 1.0
    entries = jax.random.normal(rng, dims, jnp.float32) * scale * loudness
    return jnp.minimum(jnp.maximum(entries, -bound), bound).astype(held_as)


def setup_inputs(seed: int = 0, part: int = 0) -> dict:
    seeds = jax.random.split(jax.random.key(seed), 10)
    own_keys = jax.random.split(jax.random.fold_in(seeds[9], part), 10)
    tokens = bell_draw(own_keys[0], (2, BATCH, D), 1.0, 6.0, ((1, 16),))
    positions = touch_ends(jax.random.randint(own_keys[1], (BATCH,), 0, 8192), jax.random.fold_in(own_keys[1], 1), 0, 8191).astype(jnp.int32)
    lengths = draw_lengths(jax.random.fold_in(jax.random.fold_in(seeds[9], part), 71), part)
    w_query = bell_draw(seeds[3], (D, HEADS * HEAD), D ** -0.5, 0.0625, ((1, 16),))
    w_key = bell_draw(seeds[4], (D, KV_HEADS * HEAD), D ** -0.5, 0.0625, ((1, 16),))
    w_value = bell_draw(seeds[5], (D, KV_HEADS * HEAD), D ** -0.5, 0.0625, ((1, 16),))
    w_out = bell_draw(seeds[6], (HEADS * HEAD, D), (max(HEADS * HEAD // 512, 4)) ** -0.5, 1.5, ((0, 16),))
    cache_keys = draw_cache_keys(jax.random.fold_in(jax.random.fold_in(seeds[9], part), 71), part)
    cache_values = bell_draw(own_keys[8], (BATCH, CACHE, KV_HEADS * HEAD), 1.0, 4.0, ((0, 16),))
    return {"tokens": tokens, "positions": positions, "lengths": lengths, "w_query": w_query, "w_key": w_key, "w_value": w_value, "w_out": w_out, "cache_keys": cache_keys, "cache_values": cache_values}


def normalize(values):
    widened = values.astype(jnp.float32)
    factor = jax.lax.rsqrt(lax.optimization_barrier(jnp.mean(widened * widened, axis=-1, keepdims=True)) + 1e-06)
    return (widened * factor).astype(jnp.bfloat16)

def rotate(values, places):
    half_width = values.shape[-1] // 2
    inverse = jnp.exp(jnp.arange(half_width, dtype=jnp.float32) * (-2.0 * math.log(1000000.0) / values.shape[-1]))
    angles = places.astype(jnp.float32)[:, None, None] * inverse
    cosine = jnp.cos(angles)
    sine = jnp.sin(angles)
    first_half = values[..., :half_width]
    second_half = values[..., half_width:]
    return jnp.concatenate([first_half * cosine - second_half * sine, second_half * cosine + first_half * sine], axis=-1)

def attend(query, cache_keys, cache_values, lengths, new_keys, new_values):
    row_count = query.shape[0]
    group_size = HEADS // KV_HEADS
    grouped = query.reshape(row_count, KV_HEADS, group_size, HEAD).astype(jnp.float32)
    keys_cached = cache_keys.reshape(row_count, CACHE, KV_HEADS, HEAD).astype(jnp.float32)
    values_cached = cache_values.reshape(row_count, CACHE, KV_HEADS, HEAD).astype(jnp.float32)
    scale = HEAD ** (-0.5)
    scores_cached = jnp.einsum('rkgd,rckd->rkgc', grouped, keys_cached) * scale
    valid = jnp.arange(CACHE, dtype=jnp.int32)[None, :] < lengths[:, None]
    scores_cached = jnp.where(valid[:, None, None, :], scores_cached, -jnp.inf)
    scores_new = jnp.einsum('rkgd,rnkd->rkgn', grouped, new_keys.astype(jnp.float32)) * scale
    highest = jnp.maximum(lax.optimization_barrier(jnp.max(scores_cached, axis=-1)), lax.optimization_barrier(jnp.max(scores_new, axis=-1)))
    exp_cached = jnp.exp(scores_cached - highest[..., None])
    exp_new = jnp.exp(scores_new - highest[..., None])
    total = lax.optimization_barrier(jnp.sum(exp_cached, axis=-1)) + lax.optimization_barrier(jnp.sum(exp_new, axis=-1))
    weights_cached = (exp_cached / total[..., None]).astype(jnp.bfloat16)
    weights_new = (exp_new / total[..., None]).astype(jnp.bfloat16)
    mixed = jnp.einsum('rkgc,rckd->rkgd', weights_cached.astype(jnp.float32), values_cached)
    mixed = mixed + jnp.einsum('rkgn,rnkd->rkgd', weights_new.astype(jnp.float32), new_values.astype(jnp.float32))
    return mixed.reshape(row_count, HEADS * HEAD).astype(jnp.bfloat16)

def reference(tokens, positions, lengths, w_query, w_key, w_value, w_out, cache_keys, cache_values):
    row_count = tokens.shape[1]
    keys_new = []
    values_new = []
    results = []
    for which_step in range(2):
        normed = normalize(tokens[which_step])
        query = jnp.dot(normed, w_query, preferred_element_type=jnp.float32).astype(jnp.bfloat16)
        key_part = jnp.dot(normed, w_key, preferred_element_type=jnp.float32).astype(jnp.bfloat16)
        value_part = jnp.dot(normed, w_value, preferred_element_type=jnp.float32).astype(jnp.bfloat16)
        places = positions + which_step
        query_rot = rotate(query.reshape(row_count, HEADS, HEAD).astype(jnp.float32), places).astype(jnp.bfloat16)
        key_rot = rotate(key_part.reshape(row_count, KV_HEADS, HEAD).astype(jnp.float32), places).astype(jnp.bfloat16)
        keys_new.append(key_rot)
        values_new.append(value_part.reshape(row_count, KV_HEADS, HEAD))
        mixed = attend(query_rot, cache_keys, cache_values, lengths, jnp.stack(keys_new, axis=1), jnp.stack(values_new, axis=1))
        results.append(jnp.dot(mixed, w_out, preferred_element_type=jnp.float32).astype(jnp.bfloat16))
    return jnp.stack(results)
```

```python
import math

import jax
import jax.numpy as jnp
from jax import lax
from jax.sharding import PartitionSpec as P

HEADS = 64
KV_HEADS = 8
HEAD = 128
GROUP = HEADS // KV_HEADS


def normalize(values):
    widened = values.astype(jnp.float32)
    factor = lax.rsqrt(jnp.mean(widened * widened, axis=-1, keepdims=True) + 1e-06)
    return (widened * factor).astype(jnp.bfloat16)


def rotate(values, places):
    half_width = values.shape[-1] // 2
    inverse = jnp.exp(
        jnp.arange(half_width, dtype=jnp.float32) * (-2.0 * math.log(1000000.0) / values.shape[-1])
    )
    angles = places.astype(jnp.float32)[..., None, None] * inverse
    cosine = jnp.cos(angles)
    sine = jnp.sin(angles)
    first_half = values[..., :half_width]
    second_half = values[..., half_width:]
    return jnp.concatenate(
        [first_half * cosine - second_half * sine, second_half * cosine + first_half * sine],
        axis=-1,
    )


def per_device(
    tokens, positions, lengths, w_query, w_key, w_value, w_out, cache_keys, cache_values
):
    size = lax.axis_size("hid")
    steps, _, width = tokens.shape
    capacity = cache_keys.shape[1]
    query_width = w_query.shape[1]
    key_width = w_key.shape[1]
    normed = normalize(tokens[:, 0])
    rows = lax.all_gather(normed, "hid", axis=0, tiled=True)
    parts = [
        jnp.dot(rows, w, preferred_element_type=jnp.float32).astype(jnp.bfloat16)
        for w in (w_query, w_key, w_value)
    ]
    columns = jnp.concatenate(parts, axis=-1).reshape(size, steps, -1)
    mine = lax.all_to_all(columns, "hid", split_axis=0, concat_axis=0, tiled=True)
    mine = jnp.transpose(mine, (1, 0, 2))
    query = mine[..., :query_width].reshape(steps, HEADS, HEAD)
    key = mine[..., query_width : query_width + key_width].reshape(steps, KV_HEADS, HEAD)
    value = mine[..., query_width + key_width :].reshape(steps, KV_HEADS, HEAD)
    places = positions + jnp.arange(steps, dtype=jnp.int32)
    query = rotate(query.astype(jnp.float32), places).astype(jnp.bfloat16)
    key = rotate(key.astype(jnp.float32), places).astype(jnp.bfloat16)
    grouped = query.reshape(steps, KV_HEADS, GROUP, HEAD)
    keys_cached = cache_keys[0].reshape(capacity, KV_HEADS, HEAD)
    values_cached = cache_values[0].reshape(capacity, KV_HEADS, HEAD)
    scale = HEAD ** (-0.5)
    scores_cached = (
        jnp.einsum("skgd,ckd->kgsc", grouped, keys_cached, preferred_element_type=jnp.float32)
        * scale
    )
    valid = jnp.arange(capacity, dtype=jnp.int32) < lengths[0]
    scores_cached = jnp.where(valid, scores_cached, -jnp.inf)
    scores_new = (
        jnp.einsum("skgd,nkd->kgsn", grouped, key, preferred_element_type=jnp.float32) * scale
    )
    seen = jnp.arange(steps)[None, :] <= jnp.arange(steps)[:, None]
    scores_new = jnp.where(seen, scores_new, -jnp.inf)
    highest = jnp.maximum(jnp.max(scores_cached, axis=-1), jnp.max(scores_new, axis=-1))
    exp_cached = jnp.exp(scores_cached - highest[..., None])
    exp_new = jnp.exp(scores_new - highest[..., None])
    total = jnp.sum(exp_cached, axis=-1) + jnp.sum(exp_new, axis=-1)
    weights_cached = (exp_cached / total[..., None]).astype(jnp.bfloat16)
    weights_new = (exp_new / total[..., None]).astype(jnp.bfloat16)
    mixed = jnp.einsum(
        "kgsc,ckd->skgd", weights_cached, values_cached, preferred_element_type=jnp.float32
    )
    mixed = mixed + jnp.einsum(
        "kgsn,nkd->skgd", weights_new, value, preferred_element_type=jnp.float32
    )
    mixed = mixed.astype(jnp.bfloat16).reshape(steps, size, query_width)
    mixed = jnp.transpose(mixed, (1, 0, 2))
    heads = lax.all_to_all(mixed, "hid", split_axis=0, concat_axis=0, tiled=True)
    product = jnp.dot(
        heads.reshape(size * steps, query_width), w_out, preferred_element_type=jnp.float32
    )
    summed = lax.psum_scatter(product, "hid", scatter_dimension=0, tiled=True)
    return summed.astype(jnp.bfloat16)[:, None]


def solution(mesh):
    return jax.shard_map(
        per_device,
        mesh=mesh,
        in_specs=(
            P(None, ("groups", "hid"), None),
            P(("groups", "hid")),
            P(("groups", "hid")),
            P(None, "hid"),
            P(None, "hid"),
            P(None, "hid"),
            P("hid", None),
            P(("groups", "hid"), None, None),
            P(("groups", "hid"), None, None),
        ),
        out_specs=P(None, ("groups", "hid"), None),
        check_vma=False,
    )
```

```python
import functools
import math

import jax
import jax.numpy as jnp
from jax import lax
from jax.experimental import pallas as pl
from jax.experimental.pallas import tpu as pltpu
from jax.sharding import PartitionSpec as P

HEADS = 64
KV_HEADS = 8
HEAD = 128
STEPS = 2
CHUNKS = 8
F32 = jnp.float32
BF16 = jnp.bfloat16


def push(src, dst, send, recv, peer):
    return pltpu.make_async_remote_copy(
        src_ref=src,
        dst_ref=dst,
        send_sem=send,
        recv_sem=recv,
        device_id={"hid": peer},
        device_id_type=pl.DeviceIdType.MESH,
    )


def kernel(
    n, positions, lengths, tokens, wq_hbm, wk_hbm, wv_hbm, wo_hbm, ck_hbm, cv_hbm, out,
    wq, wk, wv, wo, ck, cv,
    x_raw, x_land, x_tmp, x_rows,
    y_rows, kv_pad, q_pack, q_send, q_land, q_wide, q_rows, k_rows, v_rows,
    m_send, m_land, a_rows,
    p_rows, p_pack, p_send, p_land, o_rows,
    load_sem, x_ss, x_rs, q_ss, q_rs, m_ss, m_rs, p_ss, p_rs,
):
    me = lax.axis_index("hid")
    wide = x_raw.shape[1]
    query_width = wq.shape[1]
    own_heads = query_width // HEAD
    head_rows = STEPS * own_heads
    key_width = wk.shape[1]
    per = HEAD // key_width
    capacity = ck.shape[0]

    loads = [
        pltpu.make_async_copy(src, dst, load_sem.at[i])
        for i, (src, dst) in enumerate(
            [(wq_hbm, wq), (wk_hbm, wk), (wv_hbm, wv), (ck_hbm.at[0], ck), (cv_hbm.at[0], cv), (wo_hbm, wo)]
        )
    ]
    for load in loads:
        load.start()

    barrier = pltpu.get_barrier_semaphore()

    @pl.loop(1, n)
    def _(k):
        pl.semaphore_signal(
            barrier, inc=1, device_id={"hid": lax.rem(me + k, n)}, device_id_type=pl.DeviceIdType.MESH
        )

    for step in range(STEPS):
        for c in range(CHUNKS):
            x_raw[STEPS * c + step : STEPS * c + step + 1, :] = tokens[
                step, :, c * wide : (c + 1) * wide
            ].astype(F32)
    raw = x_raw[...]
    squares = jnp.sum(raw * raw, axis=1, keepdims=True)
    odd = lax.broadcasted_iota(jnp.int32, squares.shape, 0) % STEPS == 1
    width = CHUNKS * wide
    mean_even = jnp.sum(jnp.where(odd, 0.0, squares), axis=0, keepdims=True) / width
    mean_odd = jnp.sum(jnp.where(odd, squares, 0.0), axis=0, keepdims=True) / width
    factor = lax.rsqrt(jnp.where(odd, mean_odd, mean_even) + 1e-06)
    x_land[me] = (raw * factor).astype(BF16)

    pl.semaphore_wait(barrier, n - 1)

    def send_all(src_of, land, ss, rs):
        @pl.loop(1, n)
        def _(k):
            peer = lax.rem(me + k, n)
            push(src_of(peer), land.at[me], ss.at[peer], rs.at[me], peer).start()

    def wait_from(s, land, ss, rs):
        @pl.when(s != me)
        def _():
            push(land.at[s], land.at[s], ss.at[s], rs.at[s], s).wait_recv()

    def wait_sends(src_of, land, ss, rs):
        @pl.loop(1, n)
        def _(k):
            peer = lax.rem(me + k, n)
            push(src_of(peer), land.at[me], ss.at[peer], rs.at[me], peer).wait_send()

    send_all(lambda peer: x_land.at[me], x_land, x_ss, x_rs)

    tile = (2 * KV_HEADS, HEAD)
    lane = lax.broadcasted_iota(jnp.int32, tile, 1)
    row = lax.broadcasted_iota(jnp.int32, tile, 0)
    place = (positions[0] + row % STEPS).astype(F32)
    inverse = jnp.exp((lane % (HEAD // 2)).astype(F32) * (-2.0 * math.log(1000000.0) / HEAD))
    angle = place * inverse
    cosine = jnp.cos(angle)
    sine = jnp.sin(angle)
    sine = jnp.where(lane < HEAD // 2, -sine, sine)

    def rotate(values):
        return values * cosine + pltpu.roll(values, HEAD // 2, 1) * sine

    kv_pad[...] = jnp.zeros_like(kv_pad)
    q_pack[...] = jnp.zeros_like(q_pack)

    for s in range(n):
        wait_from(s, x_land, x_ss, x_rs)
        x_tmp[s] = x_land[s].astype(F32)
        for c in range(CHUNKS):
            x_rows[c, STEPS * s : STEPS * (s + 1), :] = x_tmp[s, STEPS * c : STEPS * (c + 1), :]

    for load in loads[:3]:
        load.wait()
    rows = STEPS * n

    def project(c, sums):
        left = x_rows[c].astype(BF16)
        part = pl.ds(pl.multiple_of(c * wide, wide), wide)
        return tuple(
            total + jnp.dot(left, w[part, :], preferred_element_type=F32)
            for total, w in zip(sums, (wq, wk, wv))
        )

    query, key, value = lax.fori_loop(
        0,
        CHUNKS,
        project,
        (
            jnp.zeros((rows, query_width), F32),
            jnp.zeros((rows, key_width), F32),
            jnp.zeros((rows, key_width), F32),
        ),
    )
    y_rows[:, :query_width] = query
    shift = lax.rem(me, per) * key_width
    kv_pad[0, :, :key_width] = key
    kv_pad[1, :, :key_width] = value
    y_rows[:, query_width : query_width + HEAD] = pltpu.roll(kv_pad[0], shift, 1)
    y_rows[:, query_width + HEAD :] = pltpu.roll(kv_pad[1], shift, 1)
    for d in range(n):
        for j in range(own_heads + 2):
            q_pack[d, STEPS * j : STEPS * (j + 1), :] = y_rows[
                STEPS * d : STEPS * (d + 1), j * HEAD : (j + 1) * HEAD
            ]
    q_send[...] = q_pack[...].astype(BF16)
    q_land[me] = q_send[me]
    send_all(lambda peer: q_send.at[peer], q_land, q_ss, q_rs)
    wait_sends(lambda peer: x_land.at[me], x_land, x_ss, x_rs)

    k_rows[...] = jnp.zeros_like(k_rows)
    v_rows[...] = jnp.zeros_like(v_rows)
    for s in range(n):
        wait_from(s, q_land, q_ss, q_rs)
        q_wide[s] = q_land[s].astype(F32)
        q_rows[head_rows * s : head_rows * (s + 1), :] = q_wide[s, :head_rows, :]
        g = s // per
        pair = slice(STEPS * g, STEPS * (g + 1))
        k_rows[pair, :] += q_wide[s, head_rows : head_rows + STEPS, :]
        v_rows[pair, :] += q_wide[s, head_rows + STEPS : head_rows + 2 * STEPS, :]
    k_rows[...] = rotate(k_rows[...])

    for load in loads[3:5]:
        load.wait()
    group_rows = STEPS * (HEADS // KV_HEADS)
    position = lax.broadcasted_iota(jnp.int32, (group_rows, capacity), 1)
    query_step = lax.broadcasted_iota(jnp.int32, (group_rows, capacity), 0) % STEPS
    seen = (position < lengths[0]) | (
        (position >= capacity - STEPS) & (position - (capacity - STEPS) <= query_step)
    )
    last = 16
    last_row = lax.broadcasted_iota(jnp.int32, (last, HEAD), 0)
    per_dest = head_rows
    for g in range(KV_HEADS):
        lanes = slice(g * HEAD, (g + 1) * HEAD)
        for cache, fresh in ((ck, k_rows), (cv, v_rows)):
            end = cache[capacity - last : capacity, lanes].astype(F32)
            for step in range(STEPS):
                r = STEPS * g + step
                end = jnp.where(last_row == last - STEPS + step, fresh[r : r + 1, :], end)
            cache[capacity - last : capacity, lanes] = end.astype(BF16)
        q = rotate(q_rows[group_rows * g : group_rows * (g + 1), :]).astype(BF16)
        scores = lax.dot_general(
            q, ck[:, lanes], (((1,), (1,)), ((), ())), preferred_element_type=F32
        ) * (HEAD ** -0.5)
        scores = jnp.where(seen, scores, -jnp.inf)
        grown = jnp.exp(scores - jnp.max(scores, axis=1, keepdims=True))
        weights = (grown / jnp.sum(grown, axis=1, keepdims=True)).astype(BF16)
        mixed = jnp.dot(weights, cv[:, lanes], preferred_element_type=F32)
        q_rows[group_rows * g : group_rows * (g + 1), :] = mixed
    for d in range(n):
        m_send[d, :per_dest, :] = q_rows[per_dest * d : per_dest * (d + 1), :]
    m_land[me] = m_send[me]
    send_all(lambda peer: m_send.at[peer], m_land, m_ss, m_rs)
    wait_sends(lambda peer: q_send.at[peer], q_land, q_ss, q_rs)
    loads[5].wait()

    for s in range(n):
        wait_from(s, m_land, m_ss, m_rs)
        for j in range(own_heads):
            a_rows[STEPS * s : STEPS * (s + 1), j * HEAD : (j + 1) * HEAD] = m_land[
                s, STEPS * j : STEPS * (j + 1), :
            ]
    left = a_rows[...].astype(BF16)

    @pl.loop(0, CHUNKS)
    def _(c):
        part = pl.ds(pl.multiple_of(c * wide, wide), wide)
        p_rows[c] = jnp.dot(left, wo[:, part], preferred_element_type=F32)

    for d in range(n):
        for c in range(CHUNKS):
            p_pack[d, STEPS * c : STEPS * (c + 1), :] = p_rows[c, STEPS * d : STEPS * (d + 1), :]
        p_send[d] = p_pack[d].astype(BF16)
    p_land[me] = p_send[me]
    send_all(lambda peer: p_send.at[peer], p_land, p_ss, p_rs)
    wait_sends(lambda peer: m_send.at[peer], m_land, m_ss, m_rs)

    total = p_pack[me]
    for s in range(n):
        wait_from(s, p_land, p_ss, p_rs)
        total = total + jnp.where(s == me, 0.0, p_land[s].astype(F32))
    o_rows[...] = total
    for step in range(STEPS):
        for c in range(CHUNKS):
            r = STEPS * c + step
            out[step, :, c * wide : (c + 1) * wide] = o_rows[r : r + 1, :].astype(BF16)
    wait_sends(lambda peer: p_send.at[peer], p_land, p_ss, p_rs)


def per_device(
    tokens, positions, lengths, w_query, w_key, w_value, w_out, cache_keys, cache_values
):
    n = lax.axis_size("hid")
    width = tokens.shape[2]
    wide = width // CHUNKS
    packed = STEPS * CHUNKS
    query_width, key_width = w_query.shape[1], w_key.shape[1]
    own_heads = query_width // HEAD
    _, capacity, kv_width = cache_keys.shape
    rows = STEPS * n
    message = -(-STEPS * (own_heads + 2) // 16) * 16
    back = -(-STEPS * own_heads // 8) * 8
    smem = pl.BlockSpec(memory_space=pltpu.SMEM)
    vmem = pl.BlockSpec(memory_space=pltpu.VMEM)
    hbm = pl.BlockSpec(memory_space=pltpu.HBM)
    dma = pltpu.SemaphoreType.DMA
    return pl.pallas_call(
        functools.partial(kernel, n),
        out_shape=jax.ShapeDtypeStruct(tokens.shape, BF16),
        in_specs=[smem, smem, vmem] + [hbm] * 6,
        out_specs=vmem,
        scratch_shapes=[
            pltpu.VMEM(w_query.shape, BF16),
            pltpu.VMEM(w_key.shape, BF16),
            pltpu.VMEM(w_value.shape, BF16),
            pltpu.VMEM(w_out.shape, BF16),
            pltpu.VMEM((capacity, kv_width), BF16),
            pltpu.VMEM((capacity, kv_width), BF16),
            pltpu.VMEM((packed, wide), F32),
            pltpu.VMEM((n, packed, wide), BF16),
            pltpu.VMEM((n, packed, wide), F32),
            pltpu.VMEM((CHUNKS, rows, wide), F32),
            pltpu.VMEM((rows, query_width + 2 * HEAD), F32),
            pltpu.VMEM((2, rows, HEAD), F32),
            pltpu.VMEM((n, message, HEAD), F32),
            pltpu.VMEM((n, message, HEAD), BF16),
            pltpu.VMEM((n, message, HEAD), BF16),
            pltpu.VMEM((n, message, HEAD), F32),
            pltpu.VMEM((STEPS * HEADS, HEAD), F32),
            pltpu.VMEM((STEPS * KV_HEADS, HEAD), F32),
            pltpu.VMEM((STEPS * KV_HEADS, HEAD), F32),
            pltpu.VMEM((n, back, HEAD), F32),
            pltpu.VMEM((n, back, HEAD), F32),
            pltpu.VMEM((rows, query_width), F32),
            pltpu.VMEM((CHUNKS, rows, wide), F32),
            pltpu.VMEM((n, packed, wide), F32),
            pltpu.VMEM((n, packed, wide), BF16),
            pltpu.VMEM((n, packed, wide), BF16),
            pltpu.VMEM((packed, wide), F32),
            dma((6,)),
        ]
        + [dma((n,))] * 8,
        compiler_params=pltpu.CompilerParams(
            collective_id=0, has_side_effects=True, vmem_limit_bytes=56 * 2**20
        ),
    )(positions, lengths, tokens, w_query, w_key, w_value, w_out, cache_keys, cache_values)


def solution(mesh):
    return jax.shard_map(
        per_device,
        mesh=mesh,
        in_specs=(
            P(None, ("groups", "hid"), None),
            P(("groups", "hid")),
            P(("groups", "hid")),
            P(None, "hid"),
            P(None, "hid"),
            P(None, "hid"),
            P("hid", None),
            P(("groups", "hid"), None, None),
            P(("groups", "hid"), None, None),
        ),
        out_specs=P(None, ("groups", "hid"), None),
        check_vma=False,
    )
```

```python
import functools
import math

import jax
import jax.numpy as jnp
from jax import lax
from jax.experimental import pallas as pl
from jax.experimental.pallas import tpu as pltpu
from jax.sharding import PartitionSpec as P

HEADS = 64
KV_HEADS = 8
HEAD = 128
STEPS = 2
CHUNKS = 8
F32 = jnp.float32
BF16 = jnp.bfloat16


def push(src, dst, send, recv, peer):
    return pltpu.make_async_remote_copy(
        src_ref=src,
        dst_ref=dst,
        send_sem=send,
        recv_sem=recv,
        device_id={"hid": peer},
        device_id_type=pl.DeviceIdType.MESH,
    )


def kernel(
    n, positions, lengths, tokens, wq_hbm, wk_hbm, wv_hbm, wo_hbm, ck_hbm, cv_hbm, out,
    wq, wkv, wo, ck, cv,
    x_raw, x_land, x_tmp, x_rows,
    y_rows, kv_pad, q_pack, q_send, q_land, q_wide, q_rows, k_rows, v_rows,
    m_send, m_land, a_rows,
    p_rows, h_send, h_land, p_pack, p_send, p_land, o_rows,
    load_sem, x_ss, x_rs, q_ss, q_rs, m_ss, m_rs, h_ss, h_rs, p_ss, p_rs,
):
    me = lax.axis_index("hid")
    chips = n // 2
    chip, core = me // 2, lax.rem(me, 2)
    partner = chip * 2 + (1 - core)
    wide = x_raw.shape[1]
    query_width = wq.shape[1]
    own_heads = query_width // HEAD
    head_rows = STEPS * own_heads
    key_width = wkv.shape[0] // 2
    per = HEAD // key_width
    capacity = ck.shape[0]
    rows = STEPS * n
    half = rows // 2

    def device(i):
        other = i // chips
        return lax.rem(chip + i % chips, chips) * 2 + lax.rem(core + other, 2)

    loads = [
        pltpu.make_async_copy(src, dst, load_sem.at[i])
        for i, (src, dst) in enumerate(
            [
                (wq_hbm, wq),
                (wk_hbm, wkv.at[:key_width]),
                (wv_hbm, wkv.at[key_width:]),
                (ck_hbm.at[0], ck),
                (cv_hbm.at[0], cv),
                (wo_hbm, wo),
            ]
        )
    ]
    for load in loads:
        load.start()

    barrier = pltpu.get_barrier_semaphore()

    @pl.loop(1, n)
    def _(k):
        pl.semaphore_signal(
            barrier, inc=1, device_id={"hid": lax.rem(me + k, n)}, device_id_type=pl.DeviceIdType.MESH
        )

    for c in range(CHUNKS):
        x_raw[STEPS * c : STEPS * (c + 1), :] = tokens[:, c * wide : (c + 1) * wide].astype(F32)
    raw = x_raw[...]
    squares = jnp.sum(raw * raw, axis=1, keepdims=True)
    odd = lax.broadcasted_iota(jnp.int32, squares.shape, 0) % STEPS == 1
    width = CHUNKS * wide
    mean_even = jnp.sum(jnp.where(odd, 0.0, squares), axis=0, keepdims=True) / width
    mean_odd = jnp.sum(jnp.where(odd, squares, 0.0), axis=0, keepdims=True) / width
    factor = lax.rsqrt(jnp.where(odd, mean_odd, mean_even) + 1e-06)
    x_land[me] = (raw * factor).astype(BF16)

    pl.semaphore_wait(barrier, n - 1)

    def wait_recv(s, land, ss, rs):
        push(land.at[s], land.at[s], ss.at[s], rs.at[s], s).wait_recv()

    def exchange(i, src, land, ss, rs):
        peer = device(i)
        return push(src, land.at[me], ss.at[peer], rs.at[me], peer)

    def direct(peer):
        return push(x_land.at[me], x_land.at[me], x_ss.at[peer], x_rs.at[me], peer)

    def forward(s, spare):
        return push(x_land.at[s], x_land.at[s], x_ss.at[spare], x_rs.at[s], partner)

    for kc in range(1, chips):
        direct(device(kc)).start()
    direct(partner).start()

    tile = (2 * KV_HEADS, HEAD)
    lane = lax.broadcasted_iota(jnp.int32, tile, 1)
    row = lax.broadcasted_iota(jnp.int32, tile, 0)
    place = (positions[0] + row % STEPS).astype(F32)
    inverse = jnp.exp((lane % (HEAD // 2)).astype(F32) * (-2.0 * math.log(1000000.0) / HEAD))
    angle = place * inverse
    cosine = jnp.cos(angle)
    sine = jnp.sin(angle)
    sine = jnp.where(lane < HEAD // 2, -sine, sine)

    def rotate(values):
        return values * cosine + pltpu.roll(values, HEAD // 2, 1) * sine

    kv_pad[...] = jnp.zeros_like(kv_pad)
    q_pack[...] = jnp.zeros_like(q_pack)

    def unpack(i):
        x_tmp[i] = x_land[device(i)].astype(F32)
        for c in range(CHUNKS):
            x_rows[c, STEPS * i : STEPS * (i + 1), :] = x_tmp[i, STEPS * c : STEPS * (c + 1), :]

    unpack(0)
    for kc in range(chips - 1, 0, -1):
        s = device(kc)
        wait_recv(s, x_land, x_ss, x_rs)
        forward(s, device(kc + chips)).start()
        unpack(kc)
    for kc in [0] + list(range(chips - 1, 0, -1)):
        wait_recv(device(kc + chips), x_land, x_ss, x_rs)
        unpack(kc + chips)

    for load in loads[:3]:
        load.wait()

    def project(c, sums):
        left = x_rows[c].astype(BF16)
        part = pl.ds(pl.multiple_of(c * wide, wide), wide)
        query = sums[0] + jnp.dot(left, wq[part, :], preferred_element_type=F32)
        fresh = sums[1] + lax.dot_general(
            left, wkv[:, part], (((1,), (1,)), ((), ())), preferred_element_type=F32
        )
        return query, fresh

    query, fresh = lax.fori_loop(
        0,
        CHUNKS,
        project,
        (jnp.zeros((rows, query_width), F32), jnp.zeros((rows, 2 * key_width), F32)),
    )
    y_rows[:, :query_width] = query
    kv_pad[:, : 2 * key_width] = fresh
    spot = lax.rem(me, per)
    both = kv_pad[...]
    here = lax.broadcasted_iota(jnp.int32, both.shape, 1) // key_width == spot
    key = pltpu.roll(both, spot * key_width, 1)
    value = pltpu.roll(both, lax.rem(spot + per - 1, per) * key_width, 1)
    y_rows[:, query_width : query_width + HEAD] = jnp.where(here, key, 0.0)
    y_rows[:, query_width + HEAD :] = jnp.where(here, value, 0.0)
    for i in range(n):
        for j in range(own_heads + 2):
            q_pack[i, STEPS * j : STEPS * (j + 1), :] = y_rows[
                STEPS * i : STEPS * (i + 1), j * HEAD : (j + 1) * HEAD
            ]
    q_send[...] = q_pack[...].astype(BF16)
    for i in range(1, n):
        exchange(i, q_send.at[i], q_land, q_ss, q_rs).start()
    q_land[me] = q_send[0]
    for kc in range(1, chips):
        direct(device(kc)).wait_send()
        forward(device(kc), device(kc + chips)).wait_send()
    direct(partner).wait_send()

    k_rows[...] = jnp.zeros_like(k_rows)
    v_rows[...] = jnp.zeros_like(v_rows)
    for load in loads[3:5]:
        load.wait()
    for i in range(1, n):
        wait_recv(device(i), q_land, q_ss, q_rs)
    for s in range(n):
        q_wide[s] = q_land[s].astype(F32)
        q_rows[head_rows * s : head_rows * (s + 1), :] = q_wide[s, :head_rows, :]
        g = s // per
        pair = slice(STEPS * g, STEPS * (g + 1))
        k_rows[pair, :] += q_wide[s, head_rows : head_rows + STEPS, :]
        v_rows[pair, :] += q_wide[s, head_rows + STEPS : head_rows + 2 * STEPS, :]
    k_rows[...] = rotate(k_rows[...])

    group_rows = STEPS * (HEADS // KV_HEADS)
    position = lax.broadcasted_iota(jnp.int32, (group_rows, capacity), 1)
    query_step = lax.broadcasted_iota(jnp.int32, (group_rows, capacity), 0) % STEPS
    seen = (position < lengths[0]) | (
        (position >= capacity - STEPS) & (position - (capacity - STEPS) <= query_step)
    )
    last = 16
    last_row = lax.broadcasted_iota(jnp.int32, (last, HEAD), 0)
    heads = [slice(g * HEAD, (g + 1) * HEAD) for g in range(KV_HEADS)]
    groups = [slice(g * group_rows, (g + 1) * group_rows) for g in range(KV_HEADS)]
    for g, lanes in enumerate(heads):
        for cache, new in ((ck, k_rows), (cv, v_rows)):
            end = cache[capacity - last : capacity, lanes].astype(F32)
            for step in range(STEPS):
                r = STEPS * g + step
                end = jnp.where(last_row == last - STEPS + step, new[r : r + 1, :], end)
            cache[capacity - last : capacity, lanes] = end.astype(BF16)
    turned = [rotate(q_rows[group, :]).astype(BF16) for group in groups]
    scores = [
        lax.dot_general(
            q, ck[:, lanes], (((1,), (1,)), ((), ())), preferred_element_type=F32
        )
        for q, lanes in zip(turned, heads)
    ]
    scores = [jnp.where(seen, score * (HEAD ** -0.5), -jnp.inf) for score in scores]
    highest = [jnp.max(score, axis=1, keepdims=True) for score in scores]
    grown = [jnp.exp(score - high) for score, high in zip(scores, highest)]
    totals = [jnp.sum(part, axis=1, keepdims=True) for part in grown]
    weights = [(part / total).astype(BF16) for part, total in zip(grown, totals)]
    mixed = [
        jnp.dot(weight, cv[:, lanes], preferred_element_type=F32)
        for weight, lanes in zip(weights, heads)
    ]
    per_group = n // KV_HEADS
    for g in range(KV_HEADS):
        for t in range(per_group):
            m_send[g * per_group + t, :head_rows, :] = mixed[g][
                head_rows * t : head_rows * (t + 1), :
            ]
    for i in range(1, n):
        exchange(i, m_send.at[device(i)], m_land, m_ss, m_rs).start()
    m_land[me] = m_send[me]
    for i in range(1, n):
        exchange(i, q_send.at[i], q_land, q_ss, q_rs).wait_send()
    loads[5].wait()

    for i in [0] + list(range(n - 1, 0, -1)):
        s = device(i)
        if i:
            wait_recv(s, m_land, m_ss, m_rs)
    for s in range(n):
        for j in range(own_heads):
            a_rows[s * STEPS : (s + 1) * STEPS, j * HEAD : (j + 1) * HEAD] = m_land[
                device(s), STEPS * j : STEPS * (j + 1), :
            ]
    left = a_rows[...].astype(BF16)

    def halve(c):
        return push(h_send.at[c], h_land.at[c], h_ss.at[c], h_rs.at[c], partner)

    for c in range(CHUNKS):
        part = jnp.dot(left, wo[:, c * wide : (c + 1) * wide], preferred_element_type=F32)
        h_send[c] = part[half:, :].astype(BF16)
        halve(c).start()
        p_rows[c] = part[:half, :]
    for c in range(CHUNKS):
        halve(c).wait_recv()
        p_rows[c] = p_rows[c] + h_land[c].astype(F32)
        for kc in range(chips):
            p_pack[kc, STEPS * c : STEPS * (c + 1), :] = p_rows[c, STEPS * kc : STEPS * (kc + 1), :]

    def reduce(kc):
        peer = device(kc)
        return push(p_send.at[kc], p_land.at[chip], p_ss.at[kc], p_rs.at[chip], peer)

    for kc in range(1, chips):
        p_send[kc] = p_pack[kc].astype(BF16)
        reduce(kc).start()
    for i in range(1, n):
        exchange(i, m_send.at[device(i)], m_land, m_ss, m_rs).wait_send()

    o_rows[...] = p_pack[0]
    for kc in range(chips - 1, 0, -1):
        s = lax.rem(chip + kc, chips)
        push(p_land.at[s], p_land.at[s], p_ss.at[kc], p_rs.at[s], device(kc)).wait_recv()
        o_rows[...] += p_land[s].astype(F32)
    for c in range(CHUNKS):
        out[:, c * wide : (c + 1) * wide] = o_rows[STEPS * c : STEPS * (c + 1), :].astype(BF16)
    for c in range(CHUNKS):
        halve(c).wait_send()
    for kc in range(1, chips):
        reduce(kc).wait_send()


def per_device(
    tokens, positions, lengths, w_query, w_key, w_value, w_out, cache_keys, cache_values
):
    n = lax.axis_size("hid")
    width = tokens.shape[2]
    wide = width // CHUNKS
    packed = STEPS * CHUNKS
    query_width, key_width = w_query.shape[1], w_key.shape[1]
    own_heads = query_width // HEAD
    _, capacity, kv_width = cache_keys.shape
    rows = STEPS * n
    message = -(-STEPS * (own_heads + 2) // 16) * 16
    back = -(-STEPS * own_heads // 8) * 8
    smem = pl.BlockSpec(memory_space=pltpu.SMEM)
    vmem = pl.BlockSpec(memory_space=pltpu.VMEM)
    hbm = pl.BlockSpec(memory_space=pltpu.HBM)
    dma = pltpu.SemaphoreType.DMA
    chips = n // 2
    result = pl.pallas_call(
        functools.partial(kernel, n),
        out_shape=jax.ShapeDtypeStruct((STEPS, width), BF16),
        in_specs=[smem, smem, vmem] + [hbm] * 6,
        out_specs=vmem,
        scratch_shapes=[
            pltpu.VMEM(w_query.shape, BF16),
            pltpu.VMEM((2 * key_width, width), BF16),
            pltpu.VMEM(w_out.shape, BF16),
            pltpu.VMEM((capacity, kv_width), BF16),
            pltpu.VMEM((capacity, kv_width), BF16),
            pltpu.VMEM((packed, wide), F32),
            pltpu.VMEM((n, packed, wide), BF16),
            pltpu.VMEM((n, packed, wide), F32),
            pltpu.VMEM((CHUNKS, rows, wide), F32),
            pltpu.VMEM((rows, query_width + 2 * HEAD), F32),
            pltpu.VMEM((rows, HEAD), F32),
            pltpu.VMEM((n, message, HEAD), F32),
            pltpu.VMEM((n, message, HEAD), BF16),
            pltpu.VMEM((n, message, HEAD), BF16),
            pltpu.VMEM((n, message, HEAD), F32),
            pltpu.VMEM((STEPS * HEADS, HEAD), F32),
            pltpu.VMEM((STEPS * KV_HEADS, HEAD), F32),
            pltpu.VMEM((STEPS * KV_HEADS, HEAD), F32),
            pltpu.VMEM((n, back, HEAD), F32),
            pltpu.VMEM((n, back, HEAD), F32),
            pltpu.VMEM((rows, query_width), F32),
            pltpu.VMEM((CHUNKS, rows // 2, wide), F32),
            pltpu.VMEM((CHUNKS, rows // 2, wide), BF16),
            pltpu.VMEM((CHUNKS, rows // 2, wide), BF16),
            pltpu.VMEM((chips, packed, wide), F32),
            pltpu.VMEM((chips, packed, wide), BF16),
            pltpu.VMEM((chips, packed, wide), BF16),
            pltpu.VMEM((packed, wide), F32),
            dma((6,)),
        ]
        + [dma((n,))] * 6
        + [dma((CHUNKS,))] * 2
        + [dma((chips,))] * 2,
        compiler_params=pltpu.CompilerParams(
            collective_id=0, has_side_effects=True, vmem_limit_bytes=56 * 2**20
        ),
    )(
        positions,
        lengths,
        tokens.reshape(STEPS, width),
        w_query,
        w_key.T,
        w_value.T,
        w_out,
        cache_keys,
        cache_values,
    )
    return result.reshape(tokens.shape)


def solution(mesh):
    return jax.shard_map(
        per_device,
        mesh=mesh,
        in_specs=(
            P(None, ("groups", "hid"), None),
            P(("groups", "hid")),
            P(("groups", "hid")),
            P(None, "hid"),
            P(None, "hid"),
            P(None, "hid"),
            P("hid", None),
            P(("groups", "hid"), None, None),
            P(("groups", "hid"), None, None),
        ),
        out_specs=P(None, ("groups", "hid"), None),
        check_vma=False,
    )
```

```python
import functools
import math

import jax
import jax.numpy as jnp
from jax import lax
from jax.experimental import pallas as pl
from jax.experimental.pallas import tpu as pltpu
from jax.sharding import PartitionSpec as P

HEADS = 64
KV_HEADS = 8
HEAD = 128
STEPS = 2
CHUNKS = 8
F32 = jnp.float32
BF16 = jnp.bfloat16


def push(src, dst, send, recv, peer):
    return pltpu.make_async_remote_copy(
        src_ref=src,
        dst_ref=dst,
        send_sem=send,
        recv_sem=recv,
        device_id={"hid": peer},
        device_id_type=pl.DeviceIdType.MESH,
    )


def kernel(
    n, positions, lengths, tokens, wq_hbm, wk_hbm, wv_hbm, wo_hbm, ck_hbm, cv_hbm, out,
    wq, wkv, wo, ck, cv,
    x_raw, x_land, x_tmp, x_rows,
    y_rows, kv_pad, q_pack, q_send, q_land, q_wide, q_rows, k_rows, v_rows,
    m_send, m_land, a_rows,
    p_rows, h_send, h_land, p_pack, p_send, p_land, o_rows,
    load_sem, x_ss, x_rs, q_ss, q_rs, m_ss, m_rs, h_ss, h_rs, p_ss, p_rs,
):
    me = lax.axis_index("hid")
    chips = n // 2
    chip, core = me // 2, lax.rem(me, 2)
    partner = chip * 2 + (1 - core)
    wide = x_raw.shape[1]
    query_width = wq.shape[1]
    own_heads = query_width // HEAD
    head_rows = STEPS * own_heads
    key_width = wkv.shape[0] // 2
    per = HEAD // key_width
    capacity = ck.shape[0]
    rows = STEPS * n
    half = rows // 2

    loads = [
        pltpu.make_async_copy(src, dst, load_sem.at[i])
        for i, (src, dst) in enumerate(
            [
                (wq_hbm, wq),
                (wk_hbm, wkv.at[:key_width]),
                (wv_hbm, wkv.at[key_width:]),
                (ck_hbm.at[0], ck),
                (cv_hbm.at[0], cv),
                (wo_hbm, wo),
            ]
        )
    ]
    for load in loads:
        load.start()

    barrier = pltpu.get_barrier_semaphore()

    @pl.loop(1, n)
    def _(k):
        pl.semaphore_signal(
            barrier, inc=1, device_id={"hid": lax.rem(me + k, n)}, device_id_type=pl.DeviceIdType.MESH
        )

    for c in range(CHUNKS):
        x_raw[STEPS * c : STEPS * (c + 1), :] = tokens[:, c * wide : (c + 1) * wide].astype(F32)
    raw = x_raw[...]
    squares = jnp.sum(raw * raw, axis=1, keepdims=True)
    odd = lax.broadcasted_iota(jnp.int32, squares.shape, 0) % STEPS == 1
    width = CHUNKS * wide
    mean_even = jnp.sum(jnp.where(odd, 0.0, squares), axis=0, keepdims=True) / width
    mean_odd = jnp.sum(jnp.where(odd, squares, 0.0), axis=0, keepdims=True) / width
    factor = lax.rsqrt(jnp.where(odd, mean_odd, mean_even) + 1e-06)
    x_land[me] = (raw * factor).astype(BF16)

    pl.semaphore_wait(barrier, n - 1)

    def wait_recv(s, land, ss, rs):
        push(land.at[s], land.at[s], ss.at[s], rs.at[s], s).wait_recv()

    def exchange(i, src, land, ss, rs):
        peer = device(i)
        return push(src, land.at[me], ss.at[peer], rs.at[me], peer)

    def direct(peer):
        return push(x_land.at[me], x_land.at[me], x_ss.at[peer], x_rs.at[me], peer)

    def forward(s, spare):
        return push(x_land.at[s], x_land.at[s], x_ss.at[spare], x_rs.at[s], partner)

    half_chips = chips // 2
    side = lax.rem(chip, 2)
    deck = chip // 2

    def line(k, other):
        chip_at = lax.rem(deck + k, half_chips) * 2 + lax.rem(side + other, 2)
        return chip_at * 2 + core

    def across(k):
        s = line(k, 0)
        return push(x_land.at[s], x_land.at[s], x_ss.at[line(k, 1)], x_rs.at[s], line(0, 1))

    def mirror(s):
        return s + 1 - 2 * core

    for k in range(1, half_chips):
        direct(line(k, 0)).start()
    across(0).start()
    direct(partner).start()

    tile = (2 * KV_HEADS, HEAD)
    lane = lax.broadcasted_iota(jnp.int32, tile, 1)
    row = lax.broadcasted_iota(jnp.int32, tile, 0)
    place = (positions[0] + row % STEPS).astype(F32)
    inverse = jnp.exp((lane % (HEAD // 2)).astype(F32) * (-2.0 * math.log(1000000.0) / HEAD))
    angle = place * inverse
    cosine = jnp.cos(angle)
    sine = jnp.sin(angle)
    sine = jnp.where(lane < HEAD // 2, -sine, sine)

    def rotate(values):
        return values * cosine + pltpu.roll(values, HEAD // 2, 1) * sine

    kv_pad[...] = jnp.zeros_like(kv_pad)
    q_pack[...] = jnp.zeros_like(q_pack)

    def device(i):
        return line(i % half_chips, i // half_chips % 2) + i // chips * (1 - 2 * core)

    def unpack(i):
        x_tmp[i] = x_land[device(i)].astype(F32)
        for c in range(CHUNKS):
            x_rows[c, STEPS * i : STEPS * (i + 1), :] = x_tmp[i, STEPS * c : STEPS * (c + 1), :]

    order = [0] + list(range(half_chips - 1, 0, -1))
    for k in order[1:]:
        s = line(k, 0)
        wait_recv(s, x_land, x_ss, x_rs)
        across(k).start()
        forward(s, mirror(s)).start()
    unpack(0)
    for k in order:
        s = line(k, 1)
        wait_recv(s, x_land, x_ss, x_rs)
        forward(s, mirror(s)).start()
        if k:
            unpack(k)
    for k in order:
        unpack(half_chips + k)
    for k in order:
        for other in range(2):
            i = chips + other * half_chips + k
            wait_recv(device(i), x_land, x_ss, x_rs)
            unpack(i)

    for load in loads[:3]:
        load.wait()

    def project(c, sums):
        left = x_rows[c].astype(BF16)
        part = pl.ds(pl.multiple_of(c * wide, wide), wide)
        query = sums[0] + jnp.dot(left, wq[part, :], preferred_element_type=F32)
        fresh = sums[1] + lax.dot_general(
            left, wkv[:, part], (((1,), (1,)), ((), ())), preferred_element_type=F32
        )
        return query, fresh

    query, fresh = lax.fori_loop(
        0,
        CHUNKS,
        project,
        (jnp.zeros((rows, query_width), F32), jnp.zeros((rows, 2 * key_width), F32)),
    )
    y_rows[:, :query_width] = query
    kv_pad[:, : 2 * key_width] = fresh
    spot = lax.rem(me, per)
    both = kv_pad[...]
    here = lax.broadcasted_iota(jnp.int32, both.shape, 1) // key_width == spot
    key = pltpu.roll(both, spot * key_width, 1)
    value = pltpu.roll(both, lax.rem(spot + per - 1, per) * key_width, 1)
    y_rows[:, query_width : query_width + HEAD] = jnp.where(here, key, 0.0)
    y_rows[:, query_width + HEAD :] = jnp.where(here, value, 0.0)
    for i in range(n):
        for j in range(own_heads + 2):
            q_pack[i, STEPS * j : STEPS * (j + 1), :] = y_rows[
                STEPS * i : STEPS * (i + 1), j * HEAD : (j + 1) * HEAD
            ]
    q_send[...] = q_pack[...].astype(BF16)
    for i in range(1, n):
        exchange(i, q_send.at[i], q_land, q_ss, q_rs).start()
    q_land[me] = q_send[0]
    for k in range(half_chips):
        across(k).wait_send()
        if k:
            direct(line(k, 0)).wait_send()
            forward(line(k, 0), mirror(line(k, 0))).wait_send()
        forward(line(k, 1), mirror(line(k, 1))).wait_send()
    direct(partner).wait_send()

    k_rows[...] = jnp.zeros_like(k_rows)
    v_rows[...] = jnp.zeros_like(v_rows)
    for load in loads[3:5]:
        load.wait()
    for i in range(1, n):
        wait_recv(device(i), q_land, q_ss, q_rs)
    for s in range(n):
        q_wide[s] = q_land[s].astype(F32)
        q_rows[head_rows * s : head_rows * (s + 1), :] = q_wide[s, :head_rows, :]
        g = s // per
        pair = slice(STEPS * g, STEPS * (g + 1))
        k_rows[pair, :] += q_wide[s, head_rows : head_rows + STEPS, :]
        v_rows[pair, :] += q_wide[s, head_rows + STEPS : head_rows + 2 * STEPS, :]
    k_rows[...] = rotate(k_rows[...])

    group_rows = STEPS * (HEADS // KV_HEADS)
    position = lax.broadcasted_iota(jnp.int32, (group_rows, capacity), 1)
    query_step = lax.broadcasted_iota(jnp.int32, (group_rows, capacity), 0) % STEPS
    seen = (position < lengths[0]) | (
        (position >= capacity - STEPS) & (position - (capacity - STEPS) <= query_step)
    )
    last = 16
    last_row = lax.broadcasted_iota(jnp.int32, (last, HEAD), 0)
    heads = [slice(g * HEAD, (g + 1) * HEAD) for g in range(KV_HEADS)]
    groups = [slice(g * group_rows, (g + 1) * group_rows) for g in range(KV_HEADS)]
    for g, lanes in enumerate(heads):
        for cache, new in ((ck, k_rows), (cv, v_rows)):
            end = cache[capacity - last : capacity, lanes].astype(F32)
            for step in range(STEPS):
                r = STEPS * g + step
                end = jnp.where(last_row == last - STEPS + step, new[r : r + 1, :], end)
            cache[capacity - last : capacity, lanes] = end.astype(BF16)
    turned = [rotate(q_rows[group, :]).astype(BF16) for group in groups]
    scores = [
        lax.dot_general(
            q, ck[:, lanes], (((1,), (1,)), ((), ())), preferred_element_type=F32
        )
        for q, lanes in zip(turned, heads)
    ]
    scores = [jnp.where(seen, score * (HEAD ** -0.5), -jnp.inf) for score in scores]
    highest = [jnp.max(score, axis=1, keepdims=True) for score in scores]
    grown = [jnp.exp(score - high) for score, high in zip(scores, highest)]
    totals = [jnp.sum(part, axis=1, keepdims=True) for part in grown]
    weights = [(part / total).astype(BF16) for part, total in zip(grown, totals)]
    mixed = [
        jnp.dot(weight, cv[:, lanes], preferred_element_type=F32)
        for weight, lanes in zip(weights, heads)
    ]
    per_group = n // KV_HEADS
    for g in range(KV_HEADS):
        for t in range(per_group):
            m_send[g * per_group + t, :head_rows, :] = mixed[g][
                head_rows * t : head_rows * (t + 1), :
            ]
    for i in range(1, n):
        exchange(i, m_send.at[device(i)], m_land, m_ss, m_rs).start()
    m_land[me] = m_send[me]
    for i in range(1, n):
        exchange(i, q_send.at[i], q_land, q_ss, q_rs).wait_send()
    loads[5].wait()

    for i in [0] + list(range(n - 1, 0, -1)):
        s = device(i)
        if i:
            wait_recv(s, m_land, m_ss, m_rs)
    for s in range(n):
        for j in range(own_heads):
            a_rows[s * STEPS : (s + 1) * STEPS, j * HEAD : (j + 1) * HEAD] = m_land[
                device(s), STEPS * j : STEPS * (j + 1), :
            ]
    left = a_rows[...].astype(BF16)

    def halve(c):
        return push(h_send.at[c], h_land.at[c], h_ss.at[c], h_rs.at[c], partner)

    for c in range(CHUNKS):
        part = jnp.dot(left, wo[:, c * wide : (c + 1) * wide], preferred_element_type=F32)
        h_send[c] = part[half:, :].astype(BF16)
        halve(c).start()
        p_rows[c] = part[:half, :]
    for c in range(CHUNKS):
        halve(c).wait_recv()
        p_rows[c] = p_rows[c] + h_land[c].astype(F32)
        for kc in range(chips):
            p_pack[kc, STEPS * c : STEPS * (c + 1), :] = p_rows[c, STEPS * kc : STEPS * (kc + 1), :]

    def reduce(kc):
        peer = device(kc)
        return push(p_send.at[kc], p_land.at[chip], p_ss.at[kc], p_rs.at[chip], peer)

    for kc in range(1, chips):
        p_send[kc] = p_pack[kc].astype(BF16)
        reduce(kc).start()
    for i in range(1, n):
        exchange(i, m_send.at[device(i)], m_land, m_ss, m_rs).wait_send()

    o_rows[...] = p_pack[0]
    for kc in range(chips - 1, 0, -1):
        s = device(kc) // 2
        push(p_land.at[s], p_land.at[s], p_ss.at[kc], p_rs.at[s], device(kc)).wait_recv()
        o_rows[...] += p_land[s].astype(F32)
    for c in range(CHUNKS):
        out[:, c * wide : (c + 1) * wide] = o_rows[STEPS * c : STEPS * (c + 1), :].astype(BF16)
    for c in range(CHUNKS):
        halve(c).wait_send()
    for kc in range(1, chips):
        reduce(kc).wait_send()


def per_device(
    tokens, positions, lengths, w_query, w_key, w_value, w_out, cache_keys, cache_values
):
    n = lax.axis_size("hid")
    width = tokens.shape[2]
    wide = width // CHUNKS
    packed = STEPS * CHUNKS
    query_width, key_width = w_query.shape[1], w_key.shape[1]
    own_heads = query_width // HEAD
    _, capacity, kv_width = cache_keys.shape
    rows = STEPS * n
    message = -(-STEPS * (own_heads + 2) // 16) * 16
    back = -(-STEPS * own_heads // 8) * 8
    smem = pl.BlockSpec(memory_space=pltpu.SMEM)
    vmem = pl.BlockSpec(memory_space=pltpu.VMEM)
    hbm = pl.BlockSpec(memory_space=pltpu.HBM)
    dma = pltpu.SemaphoreType.DMA
    chips = n // 2
    result = pl.pallas_call(
        functools.partial(kernel, n),
        out_shape=jax.ShapeDtypeStruct((STEPS, width), BF16),
        in_specs=[smem, smem, vmem] + [hbm] * 6,
        out_specs=vmem,
        scratch_shapes=[
            pltpu.VMEM(w_query.shape, BF16),
            pltpu.VMEM((2 * key_width, width), BF16),
            pltpu.VMEM(w_out.shape, BF16),
            pltpu.VMEM((capacity, kv_width), BF16),
            pltpu.VMEM((capacity, kv_width), BF16),
            pltpu.VMEM((packed, wide), F32),
            pltpu.VMEM((n, packed, wide), BF16),
            pltpu.VMEM((n, packed, wide), F32),
            pltpu.VMEM((CHUNKS, rows, wide), F32),
            pltpu.VMEM((rows, query_width + 2 * HEAD), F32),
            pltpu.VMEM((rows, HEAD), F32),
            pltpu.VMEM((n, message, HEAD), F32),
            pltpu.VMEM((n, message, HEAD), BF16),
            pltpu.VMEM((n, message, HEAD), BF16),
            pltpu.VMEM((n, message, HEAD), F32),
            pltpu.VMEM((STEPS * HEADS, HEAD), F32),
            pltpu.VMEM((STEPS * KV_HEADS, HEAD), F32),
            pltpu.VMEM((STEPS * KV_HEADS, HEAD), F32),
            pltpu.VMEM((n, back, HEAD), F32),
            pltpu.VMEM((n, back, HEAD), F32),
            pltpu.VMEM((rows, query_width), F32),
            pltpu.VMEM((CHUNKS, rows // 2, wide), F32),
            pltpu.VMEM((CHUNKS, rows // 2, wide), BF16),
            pltpu.VMEM((CHUNKS, rows // 2, wide), BF16),
            pltpu.VMEM((chips, packed, wide), F32),
            pltpu.VMEM((chips, packed, wide), BF16),
            pltpu.VMEM((chips, packed, wide), BF16),
            pltpu.VMEM((packed, wide), F32),
            dma((6,)),
        ]
        + [dma((n,))] * 6
        + [dma((CHUNKS,))] * 2
        + [dma((chips,))] * 2,
        compiler_params=pltpu.CompilerParams(
            collective_id=0, has_side_effects=True, vmem_limit_bytes=56 * 2**20
        ),
    )(
        positions,
        lengths,
        tokens.reshape(STEPS, width),
        w_query,
        w_key.T,
        w_value.T,
        w_out,
        cache_keys,
        cache_values,
    )
    return result.reshape(tokens.shape)


def solution(mesh):
    return jax.shard_map(
        per_device,
        mesh=mesh,
        in_specs=(
            P(None, ("groups", "hid"), None),
            P(("groups", "hid")),
            P(("groups", "hid")),
            P(None, "hid"),
            P(None, "hid"),
            P(None, "hid"),
            P("hid", None),
            P(("groups", "hid"), None, None),
            P(("groups", "hid"), None, None),
        ),
        out_specs=P(None, ("groups", "hid"), None),
        check_vma=False,
    )
```

```python
import functools
import math

import jax
import jax.numpy as jnp
from jax import lax
from jax.experimental import pallas as pl
from jax.experimental.pallas import tpu as pltpu
from jax.sharding import PartitionSpec as P

HEADS = 64
KV_HEADS = 8
HEAD = 128
STEPS = 2
CHUNKS = 8
F32 = jnp.float32
BF16 = jnp.bfloat16


def push(src, dst, send, recv, peer):
    return pltpu.make_async_remote_copy(
        src_ref=src,
        dst_ref=dst,
        send_sem=send,
        recv_sem=recv,
        device_id={"hid": peer},
        device_id_type=pl.DeviceIdType.MESH,
    )


def kernel(
    n, positions, lengths, tokens_hbm, wq_hbm, wk_hbm, wv_hbm, wo_hbm, ck_hbm, cv_hbm, out,
    tokens, wq, wkv, wo, ck, cv,
    x_raw, x_land, x_tmp, x_rows,
    y_rows, kv_pad, q_pack, q_send, q_land, q_wide, q_rows, k_rows, v_rows,
    m_send, m_land, a_rows,
    p_rows, h_send, h_land, p_pack, p_send, p_land, o_rows,
    load_sem, x_ss, x_rs, q_ss, q_rs, m_ss, m_rs, h_ss, h_rs, p_ss, p_rs,
):
    me = lax.axis_index("hid")
    chips = n // 2
    chip, core = me // 2, lax.rem(me, 2)
    partner = chip * 2 + (1 - core)
    wide = x_raw.shape[1]
    query_width = wq.shape[1]
    own_heads = query_width // HEAD
    head_rows = STEPS * own_heads
    key_width = wkv.shape[0] // 2
    per = HEAD // key_width
    capacity = ck.shape[0]
    rows = STEPS * n
    half = rows // 2

    def device(i):
        other = i // chips
        return lax.rem(chip + i % chips, chips) * 2 + lax.rem(core + other, 2)

    loads = [
        pltpu.make_async_copy(src, dst, load_sem.at[i])
        for i, (src, dst) in enumerate(
            [
                (wq_hbm, wq),
                (wk_hbm, wkv.at[:key_width]),
                (wv_hbm, wkv.at[key_width:]),
                (ck_hbm.at[0], ck),
                (cv_hbm.at[0], cv),
                (wo_hbm, wo),
                (tokens_hbm, tokens),
            ]
        )
    ]
    loads[6].start()
    barrier = pltpu.get_barrier_semaphore()

    @pl.loop(1, n)
    def _(k):
        pl.semaphore_signal(
            barrier, inc=1, device_id={"hid": lax.rem(me + k, n)}, device_id_type=pl.DeviceIdType.MESH
        )

    for load in loads[:6]:
        load.start()
    loads[6].wait()

    for c in range(CHUNKS):
        x_raw[STEPS * c : STEPS * (c + 1), :] = tokens[:, c * wide : (c + 1) * wide].astype(F32)
    raw = x_raw[...]
    squares = jnp.sum(raw * raw, axis=1, keepdims=True)
    odd = lax.broadcasted_iota(jnp.int32, squares.shape, 0) % STEPS == 1
    width = CHUNKS * wide
    mean_even = jnp.sum(jnp.where(odd, 0.0, squares), axis=0, keepdims=True) / width
    mean_odd = jnp.sum(jnp.where(odd, squares, 0.0), axis=0, keepdims=True) / width
    factor = lax.rsqrt(jnp.where(odd, mean_odd, mean_even) + 1e-06)
    x_land[me] = (raw * factor).astype(BF16)

    pl.semaphore_wait(barrier, n - 1)

    def wait_recv(s, land, ss, rs):
        push(land.at[s], land.at[s], ss.at[s], rs.at[s], s).wait_recv()

    def exchange(i, src, land, ss, rs):
        peer = device(i)
        return push(src, land.at[me], ss.at[peer], rs.at[me], peer)

    def direct(peer):
        return push(x_land.at[me], x_land.at[me], x_ss.at[peer], x_rs.at[me], peer)

    def forward(s, spare):
        return push(x_land.at[s], x_land.at[s], x_ss.at[spare], x_rs.at[s], partner)

    for kc in range(1, chips):
        direct(device(kc)).start()
    direct(partner).start()

    tile = (2 * KV_HEADS, HEAD)
    lane = lax.broadcasted_iota(jnp.int32, tile, 1)
    row = lax.broadcasted_iota(jnp.int32, tile, 0)
    place = (positions[0] + row % STEPS).astype(F32)
    inverse = jnp.exp((lane % (HEAD // 2)).astype(F32) * (-2.0 * math.log(1000000.0) / HEAD))
    angle = place * inverse
    cosine = jnp.cos(angle)
    sine = jnp.sin(angle)
    sine = jnp.where(lane < HEAD // 2, -sine, sine)

    def rotate(values):
        return values * cosine + pltpu.roll(values, HEAD // 2, 1) * sine

    kv_pad[...] = jnp.zeros_like(kv_pad)
    q_pack[...] = jnp.zeros_like(q_pack)

    def unpack(i):
        x_tmp[i] = x_land[device(i)].astype(F32)
        for c in range(CHUNKS):
            x_rows[c, STEPS * i : STEPS * (i + 1), :] = x_tmp[i, STEPS * c : STEPS * (c + 1), :]

    unpack(0)
    for kc in range(chips - 1, 0, -1):
        s = device(kc)
        wait_recv(s, x_land, x_ss, x_rs)
        forward(s, device(kc + chips)).start()
        unpack(kc)
    for kc in [0] + list(range(chips - 1, 0, -1)):
        wait_recv(device(kc + chips), x_land, x_ss, x_rs)
        unpack(kc + chips)

    for load in loads[:3]:
        load.wait()

    def project(c, sums):
        left = x_rows[c].astype(BF16)
        part = pl.ds(pl.multiple_of(c * wide, wide), wide)
        query = sums[0] + jnp.dot(left, wq[part, :], preferred_element_type=F32)
        fresh = sums[1] + lax.dot_general(
            left, wkv[:, part], (((1,), (1,)), ((), ())), preferred_element_type=F32
        )
        return query, fresh

    query, fresh = lax.fori_loop(
        0,
        CHUNKS,
        project,
        (jnp.zeros((rows, query_width), F32), jnp.zeros((rows, 2 * key_width), F32)),
    )
    y_rows[:, :query_width] = query
    kv_pad[:, : 2 * key_width] = fresh
    spot = lax.rem(me, per)
    both = kv_pad[...]
    here = lax.broadcasted_iota(jnp.int32, both.shape, 1) // key_width == spot
    key = pltpu.roll(both, spot * key_width, 1)
    value = pltpu.roll(both, lax.rem(spot + per - 1, per) * key_width, 1)
    y_rows[:, query_width : query_width + HEAD] = jnp.where(here, key, 0.0)
    y_rows[:, query_width + HEAD :] = jnp.where(here, value, 0.0)
    for i in range(n):
        for j in range(own_heads + 2):
            q_pack[i, STEPS * j : STEPS * (j + 1), :] = y_rows[
                STEPS * i : STEPS * (i + 1), j * HEAD : (j + 1) * HEAD
            ]
    q_send[...] = q_pack[...].astype(BF16)
    for i in range(1, n):
        exchange(i, q_send.at[i], q_land, q_ss, q_rs).start()
    q_land[me] = q_send[0]
    for kc in range(1, chips):
        direct(device(kc)).wait_send()
        forward(device(kc), device(kc + chips)).wait_send()
    direct(partner).wait_send()

    k_rows[...] = jnp.zeros_like(k_rows)
    v_rows[...] = jnp.zeros_like(v_rows)
    for load in loads[3:5]:
        load.wait()
    for i in range(1, n):
        wait_recv(device(i), q_land, q_ss, q_rs)
    for s in range(n):
        q_wide[s] = q_land[s].astype(F32)
        q_rows[head_rows * s : head_rows * (s + 1), :] = q_wide[s, :head_rows, :]
        g = s // per
        pair = slice(STEPS * g, STEPS * (g + 1))
        k_rows[pair, :] += q_wide[s, head_rows : head_rows + STEPS, :]
        v_rows[pair, :] += q_wide[s, head_rows + STEPS : head_rows + 2 * STEPS, :]
    k_rows[...] = rotate(k_rows[...])

    group_rows = STEPS * (HEADS // KV_HEADS)
    position = lax.broadcasted_iota(jnp.int32, (group_rows, capacity), 1)
    query_step = lax.broadcasted_iota(jnp.int32, (group_rows, capacity), 0) % STEPS
    seen = (position < lengths[0]) | (
        (position >= capacity - STEPS) & (position - (capacity - STEPS) <= query_step)
    )
    last = 16
    last_row = lax.broadcasted_iota(jnp.int32, (last, HEAD), 0)
    heads = [slice(g * HEAD, (g + 1) * HEAD) for g in range(KV_HEADS)]
    groups = [slice(g * group_rows, (g + 1) * group_rows) for g in range(KV_HEADS)]
    for g, lanes in enumerate(heads):
        for cache, new in ((ck, k_rows), (cv, v_rows)):
            end = cache[capacity - last : capacity, lanes].astype(F32)
            for step in range(STEPS):
                r = STEPS * g + step
                end = jnp.where(last_row == last - STEPS + step, new[r : r + 1, :], end)
            cache[capacity - last : capacity, lanes] = end.astype(BF16)
    turned = [rotate(q_rows[group, :]).astype(BF16) for group in groups]
    scores = [
        lax.dot_general(
            q, ck[:, lanes], (((1,), (1,)), ((), ())), preferred_element_type=F32
        )
        for q, lanes in zip(turned, heads)
    ]
    scores = [jnp.where(seen, score * (HEAD ** -0.5), -jnp.inf) for score in scores]
    highest = [jnp.max(score, axis=1, keepdims=True) for score in scores]
    grown = [jnp.exp(score - high) for score, high in zip(scores, highest)]
    totals = [jnp.sum(part, axis=1, keepdims=True) for part in grown]
    weights = [(part / total).astype(BF16) for part, total in zip(grown, totals)]
    mixed = [
        jnp.dot(weight, cv[:, lanes], preferred_element_type=F32)
        for weight, lanes in zip(weights, heads)
    ]
    per_group = n // KV_HEADS
    for g in range(KV_HEADS):
        for t in range(per_group):
            m_send[g * per_group + t, :head_rows, :] = mixed[g][
                head_rows * t : head_rows * (t + 1), :
            ]
    for i in range(1, n):
        exchange(i, m_send.at[device(i)], m_land, m_ss, m_rs).start()
    m_land[me] = m_send[me]
    for i in range(1, n):
        exchange(i, q_send.at[i], q_land, q_ss, q_rs).wait_send()
    loads[5].wait()

    for i in [0] + list(range(n - 1, 0, -1)):
        s = device(i)
        if i:
            wait_recv(s, m_land, m_ss, m_rs)
    for s in range(n):
        for j in range(own_heads):
            a_rows[s * STEPS : (s + 1) * STEPS, j * HEAD : (j + 1) * HEAD] = m_land[
                device(s), STEPS * j : STEPS * (j + 1), :
            ]
    left = a_rows[...].astype(BF16)

    def halve(c):
        return push(h_send.at[c], h_land.at[c], h_ss.at[c], h_rs.at[c], partner)

    for c in range(CHUNKS):
        part = jnp.dot(left, wo[:, c * wide : (c + 1) * wide], preferred_element_type=F32)
        h_send[c] = part[half:, :].astype(BF16)
        halve(c).start()
        p_rows[c] = part[:half, :]
    for c in range(CHUNKS):
        halve(c).wait_recv()
        p_rows[c] = p_rows[c] + h_land[c].astype(F32)
        for kc in range(chips):
            p_pack[kc, STEPS * c : STEPS * (c + 1), :] = p_rows[c, STEPS * kc : STEPS * (kc + 1), :]

    def reduce(kc):
        peer = device(kc)
        return push(p_send.at[kc], p_land.at[chip], p_ss.at[kc], p_rs.at[chip], peer)

    for kc in range(1, chips):
        p_send[kc] = p_pack[kc].astype(BF16)
        reduce(kc).start()
    for i in range(1, n):
        exchange(i, m_send.at[device(i)], m_land, m_ss, m_rs).wait_send()

    o_rows[...] = p_pack[0]
    for kc in range(chips - 1, 0, -1):
        s = lax.rem(chip + kc, chips)
        push(p_land.at[s], p_land.at[s], p_ss.at[kc], p_rs.at[s], device(kc)).wait_recv()
        o_rows[...] += p_land[s].astype(F32)
    for c in range(CHUNKS):
        out[:, c * wide : (c + 1) * wide] = o_rows[STEPS * c : STEPS * (c + 1), :].astype(BF16)
    for c in range(CHUNKS):
        halve(c).wait_send()
    for kc in range(1, chips):
        reduce(kc).wait_send()


def per_device(
    tokens, positions, lengths, w_query, w_key, w_value, w_out, cache_keys, cache_values
):
    n = lax.axis_size("hid")
    width = tokens.shape[2]
    wide = width // CHUNKS
    packed = STEPS * CHUNKS
    query_width, key_width = w_query.shape[1], w_key.shape[1]
    own_heads = query_width // HEAD
    _, capacity, kv_width = cache_keys.shape
    rows = STEPS * n
    message = -(-STEPS * (own_heads + 2) // 16) * 16
    back = -(-STEPS * own_heads // 8) * 8
    smem = pl.BlockSpec(memory_space=pltpu.SMEM)
    vmem = pl.BlockSpec(memory_space=pltpu.VMEM)
    hbm = pl.BlockSpec(memory_space=pltpu.HBM)
    dma = pltpu.SemaphoreType.DMA
    chips = n // 2
    result = pl.pallas_call(
        functools.partial(kernel, n),
        out_shape=pltpu.VMEM((STEPS, width), BF16),
        in_specs=[smem, smem] + [hbm] * 7,
        out_specs=vmem,
        scratch_shapes=[
            pltpu.VMEM((STEPS, width), BF16),
            pltpu.VMEM(w_query.shape, BF16),
            pltpu.VMEM((2 * key_width, width), BF16),
            pltpu.VMEM(w_out.shape, BF16),
            pltpu.VMEM((capacity, kv_width), BF16),
            pltpu.VMEM((capacity, kv_width), BF16),
            pltpu.VMEM((packed, wide), F32),
            pltpu.VMEM((n, packed, wide), BF16),
            pltpu.VMEM((n, packed, wide), F32),
            pltpu.VMEM((CHUNKS, rows, wide), F32),
            pltpu.VMEM((rows, query_width + 2 * HEAD), F32),
            pltpu.VMEM((rows, HEAD), F32),
            pltpu.VMEM((n, message, HEAD), F32),
            pltpu.VMEM((n, message, HEAD), BF16),
            pltpu.VMEM((n, message, HEAD), BF16),
            pltpu.VMEM((n, message, HEAD), F32),
            pltpu.VMEM((STEPS * HEADS, HEAD), F32),
            pltpu.VMEM((STEPS * KV_HEADS, HEAD), F32),
            pltpu.VMEM((STEPS * KV_HEADS, HEAD), F32),
            pltpu.VMEM((n, back, HEAD), F32),
            pltpu.VMEM((n, back, HEAD), F32),
            pltpu.VMEM((rows, query_width), F32),
            pltpu.VMEM((CHUNKS, rows // 2, wide), F32),
            pltpu.VMEM((CHUNKS, rows // 2, wide), BF16),
            pltpu.VMEM((CHUNKS, rows // 2, wide), BF16),
            pltpu.VMEM((chips, packed, wide), F32),
            pltpu.VMEM((chips, packed, wide), BF16),
            pltpu.VMEM((chips, packed, wide), BF16),
            pltpu.VMEM((packed, wide), F32),
            dma((7,)),
        ]
        + [dma((n,))] * 6
        + [dma((CHUNKS,))] * 2
        + [dma((chips,))] * 2,
        compiler_params=pltpu.CompilerParams(
            collective_id=0, has_side_effects=True, vmem_limit_bytes=56 * 2**20
        ),
    )(
        positions,
        lengths,
        tokens.reshape(STEPS, width),
        w_query,
        w_key.T,
        w_value.T,
        w_out,
        cache_keys,
        cache_values,
    )
    return result.reshape(tokens.shape)


def solution(mesh):
    return jax.shard_map(
        per_device,
        mesh=mesh,
        in_specs=(
            P(None, ("groups", "hid"), None),
            P(("groups", "hid")),
            P(("groups", "hid")),
            P(None, "hid"),
            P(None, "hid"),
            P(None, "hid"),
            P("hid", None),
            P(("groups", "hid"), None, None),
            P(("groups", "hid"), None, None),
        ),
        out_specs=P(None, ("groups", "hid"), None),
        check_vma=False,
    )
```

```python
import functools
import math

import jax
import jax.numpy as jnp
from jax import lax
from jax.experimental import pallas as pl
from jax.experimental.pallas import tpu as pltpu
from jax.sharding import PartitionSpec as P

HEADS = 64
KV_HEADS = 8
HEAD = 128
STEPS = 2
CHUNKS = 8
F32 = jnp.float32
BF16 = jnp.bfloat16


def push(src, dst, send, recv, peer):
    return pltpu.make_async_remote_copy(
        src_ref=src,
        dst_ref=dst,
        send_sem=send,
        recv_sem=recv,
        device_id={"hid": peer},
        device_id_type=pl.DeviceIdType.MESH,
    )


def kernel(
    n, positions, lengths, tokens_hbm, wq_hbm, wk_hbm, wv_hbm, wo_hbm, ck_hbm, cv_hbm, out,
    tokens, wq, wkv, wo, ck, cv,
    x_raw, x_land, x_tmp, x_rows,
    y_rows, kv_pad, q_pack, q_send, q_land, q_wide, q_rows, k_rows, v_rows,
    m_send, m_land, a_rows,
    p_rows, h_send, h_land, p_pack, p_send, p_land, o_rows,
    load_sem, x_ss, x_rs, q_ss, q_rs, m_ss, m_rs, h_ss, h_rs, p_ss, p_rs,
):
    me = lax.axis_index("hid")
    chips = n // 2
    chip, core = me // 2, lax.rem(me, 2)
    partner = chip * 2 + (1 - core)
    wide = x_raw.shape[1]
    query_width = wq.shape[1]
    own_heads = query_width // HEAD
    head_rows = STEPS * own_heads
    key_width = wkv.shape[0] // 2
    per = HEAD // key_width
    capacity = ck.shape[0]
    rows = STEPS * n
    half = rows // 2

    def device(i):
        other = i // chips
        return lax.rem(chip + i % chips, chips) * 2 + lax.rem(core + other, 2)

    loads = [
        pltpu.make_async_copy(src, dst, load_sem.at[i])
        for i, (src, dst) in enumerate(
            [
                (wq_hbm, wq),
                (wk_hbm, wkv.at[:key_width]),
                (wv_hbm, wkv.at[key_width:]),
                (ck_hbm.at[0], ck),
                (cv_hbm.at[0], cv),
                (wo_hbm, wo),
                (tokens_hbm, tokens),
            ]
        )
    ]
    loads[6].start()
    barrier = pltpu.get_barrier_semaphore()

    @pl.loop(1, n)
    def _(k):
        pl.semaphore_signal(
            barrier, inc=1, device_id={"hid": lax.rem(me + k, n)}, device_id_type=pl.DeviceIdType.MESH
        )

    for load in loads[:6]:
        load.start()
    loads[6].wait()

    for c in range(CHUNKS):
        x_raw[STEPS * c : STEPS * (c + 1), :] = tokens[:, c * wide : (c + 1) * wide].astype(F32)
    raw = x_raw[...]
    squares = jnp.sum(raw * raw, axis=1, keepdims=True)
    odd = lax.broadcasted_iota(jnp.int32, squares.shape, 0) % STEPS == 1
    width = CHUNKS * wide
    mean_even = jnp.sum(jnp.where(odd, 0.0, squares), axis=0, keepdims=True) / width
    mean_odd = jnp.sum(jnp.where(odd, squares, 0.0), axis=0, keepdims=True) / width
    factor = lax.rsqrt(jnp.where(odd, mean_odd, mean_even) + 1e-06)
    x_land[me] = (raw * factor).astype(BF16)

    pl.semaphore_wait(barrier, n - 1)

    def wait_recv(s, land, ss, rs):
        push(land.at[s], land.at[s], ss.at[s], rs.at[s], s).wait_recv()

    def exchange(i, src, land, ss, rs):
        peer = device(i)
        return push(src, land.at[me], ss.at[peer], rs.at[me], peer)

    def direct(peer):
        return push(x_land.at[me], x_land.at[me], x_ss.at[peer], x_rs.at[me], peer)

    def forward(s, spare):
        return push(x_land.at[s], x_land.at[s], x_ss.at[spare], x_rs.at[s], partner)

    for kc in range(1, chips):
        direct(device(kc)).start()
    direct(partner).start()

    tile = (2 * KV_HEADS, HEAD)
    lane = lax.broadcasted_iota(jnp.int32, tile, 1)
    row = lax.broadcasted_iota(jnp.int32, tile, 0)
    place = (positions[0] + row % STEPS).astype(F32)
    inverse = jnp.exp((lane % (HEAD // 2)).astype(F32) * (-2.0 * math.log(1000000.0) / HEAD))
    angle = place * inverse
    cosine = jnp.cos(angle)
    sine = jnp.sin(angle)
    sine = jnp.where(lane < HEAD // 2, -sine, sine)

    def rotate(values):
        return values * cosine + pltpu.roll(values, HEAD // 2, 1) * sine

    kv_pad[...] = jnp.zeros_like(kv_pad)
    q_pack[...] = jnp.zeros_like(q_pack)

    def unpack(i):
        x_tmp[i] = x_land[device(i)].astype(F32)
        for c in range(CHUNKS):
            x_rows[c, STEPS * i : STEPS * (i + 1), :] = x_tmp[i, STEPS * c : STEPS * (c + 1), :]

    unpack(0)
    for kc in range(chips - 1, 0, -1):
        s = device(kc)
        wait_recv(s, x_land, x_ss, x_rs)
        forward(s, device(kc + chips)).start()
        unpack(kc)
    for kc in [0] + list(range(chips - 1, 0, -1)):
        wait_recv(device(kc + chips), x_land, x_ss, x_rs)
        unpack(kc + chips)

    for load in loads[:3]:
        load.wait()

    def project(c, sums):
        left = x_rows[c].astype(BF16)
        part = pl.ds(pl.multiple_of(c * wide, wide), wide)
        query = sums[0] + jnp.dot(left, wq[part, :], preferred_element_type=F32)
        fresh = sums[1] + lax.dot_general(
            left, wkv[:, part], (((1,), (1,)), ((), ())), preferred_element_type=F32
        )
        return query, fresh

    query, fresh = lax.fori_loop(
        0,
        CHUNKS,
        project,
        (jnp.zeros((rows, query_width), F32), jnp.zeros((rows, 2 * key_width), F32)),
    )
    y_rows[:, :query_width] = query
    kv_pad[:, : 2 * key_width] = fresh
    spot = lax.rem(me, per)
    both = kv_pad[...]
    here = lax.broadcasted_iota(jnp.int32, both.shape, 1) // key_width == spot
    key = pltpu.roll(both, spot * key_width, 1)
    value = pltpu.roll(both, lax.rem(spot + per - 1, per) * key_width, 1)
    y_rows[:, query_width : query_width + HEAD] = jnp.where(here, key, 0.0)
    y_rows[:, query_width + HEAD :] = jnp.where(here, value, 0.0)
    for i in range(n):
        for j in range(own_heads + 2):
            q_pack[i, STEPS * j : STEPS * (j + 1), :] = y_rows[
                STEPS * i : STEPS * (i + 1), j * HEAD : (j + 1) * HEAD
            ]
    q_send[...] = q_pack[...].astype(BF16)
    for i in range(1, n):
        exchange(i, q_send.at[i], q_land, q_ss, q_rs).start()
    q_land[me] = q_send[0]
    for kc in range(1, chips):
        direct(device(kc)).wait_send()
        forward(device(kc), device(kc + chips)).wait_send()
    direct(partner).wait_send()

    k_rows[...] = jnp.zeros_like(k_rows)
    v_rows[...] = jnp.zeros_like(v_rows)
    for load in loads[3:5]:
        load.wait()
    for i in range(1, n):
        wait_recv(device(i), q_land, q_ss, q_rs)
    for s in range(n):
        q_wide[s] = q_land[s].astype(F32)
        q_rows[head_rows * s : head_rows * (s + 1), :] = q_wide[s, :head_rows, :]
        g = s // per
        pair = slice(STEPS * g, STEPS * (g + 1))
        k_rows[pair, :] += q_wide[s, head_rows : head_rows + STEPS, :]
        v_rows[pair, :] += q_wide[s, head_rows + STEPS : head_rows + 2 * STEPS, :]
    k_rows[...] = rotate(k_rows[...])

    group_rows = STEPS * (HEADS // KV_HEADS)
    position = lax.broadcasted_iota(jnp.int32, (group_rows, capacity), 1)
    query_step = lax.broadcasted_iota(jnp.int32, (group_rows, capacity), 0) % STEPS
    seen = (position < lengths[0]) | (
        (position >= capacity - STEPS) & (position - (capacity - STEPS) <= query_step)
    )
    last = 16
    last_row = lax.broadcasted_iota(jnp.int32, (last, HEAD), 0)
    heads = [slice(g * HEAD, (g + 1) * HEAD) for g in range(KV_HEADS)]
    groups = [slice(g * group_rows, (g + 1) * group_rows) for g in range(KV_HEADS)]
    for g, lanes in enumerate(heads):
        for cache, new in ((ck, k_rows), (cv, v_rows)):
            end = cache[capacity - last : capacity, lanes].astype(F32)
            for step in range(STEPS):
                r = STEPS * g + step
                end = jnp.where(last_row == last - STEPS + step, new[r : r + 1, :], end)
            cache[capacity - last : capacity, lanes] = end.astype(BF16)
    turned = [rotate(q_rows[group, :]).astype(BF16) for group in groups]
    scores = [
        lax.dot_general(
            q, ck[:, lanes], (((1,), (1,)), ((), ())), preferred_element_type=F32
        )
        for q, lanes in zip(turned, heads)
    ]
    scores = [jnp.where(seen, score * (HEAD ** -0.5), -jnp.inf) for score in scores]
    highest = [jnp.max(score, axis=1, keepdims=True) for score in scores]
    grown = [jnp.exp(score - high) for score, high in zip(scores, highest)]
    totals = [jnp.sum(part, axis=1, keepdims=True) for part in grown]
    weights = [(part / total).astype(BF16) for part, total in zip(grown, totals)]
    mixed = [
        jnp.dot(weight, cv[:, lanes], preferred_element_type=F32)
        for weight, lanes in zip(weights, heads)
    ]
    per_group = n // KV_HEADS
    for g in range(KV_HEADS):
        for t in range(per_group):
            m_send[g * per_group + t, :head_rows, :] = mixed[g][
                head_rows * t : head_rows * (t + 1), :
            ]
    for i in range(1, n):
        exchange(i, m_send.at[device(i)], m_land, m_ss, m_rs).start()
    m_land[me] = m_send[me]
    for i in range(1, n):
        exchange(i, q_send.at[i], q_land, q_ss, q_rs).wait_send()
    loads[5].wait()

    for i in [0] + list(range(n - 1, 0, -1)):
        s = device(i)
        if i:
            wait_recv(s, m_land, m_ss, m_rs)
    for s in range(n):
        for j in range(own_heads):
            a_rows[s * STEPS : (s + 1) * STEPS, j * HEAD : (j + 1) * HEAD] = m_land[
                device(s), STEPS * j : STEPS * (j + 1), :
            ]
    left = a_rows[...].astype(BF16)

    def halve(c):
        return push(h_send.at[c], h_land.at[c], h_ss.at[c], h_rs.at[c], partner)

    for c in range(CHUNKS):
        part = jnp.dot(left, wo[:, c * wide : (c + 1) * wide], preferred_element_type=F32)
        h_send[c] = part[half:, :].astype(BF16)
        halve(c).start()
        p_rows[c] = part[:half, :]
    slim = wide // 2
    per_part = CHUNKS // 2

    def reduce(h, kc):
        peer = device(kc)
        to, at = h * chips + kc, h * chips + chip
        return push(p_send.at[h, kc], p_land.at[h, chip], p_ss.at[to], p_rs.at[at], peer)

    for h in range(2):
        for c in range(h * per_part, (h + 1) * per_part):
            halve(c).wait_recv()
            p_rows[c] = p_rows[c] + h_land[c].astype(F32)
            for t in range(2):
                r = STEPS * (2 * (c - h * per_part) + t)
                for kc in range(chips):
                    p_pack[h, kc, r : r + STEPS, :] = p_rows[
                        c, STEPS * kc : STEPS * (kc + 1), t * slim : (t + 1) * slim
                    ]
        for kc in range(1, chips):
            p_send[h, kc] = p_pack[h, kc].astype(BF16)
            reduce(h, kc).start()
    for i in range(1, n):
        exchange(i, m_send.at[device(i)], m_land, m_ss, m_rs).wait_send()

    for h in range(2):
        total = p_pack[h, 0]
        for kc in range(chips - 1, 0, -1):
            s = lax.rem(chip + kc, chips)
            to, at = h * chips + kc, h * chips + s
            push(
                p_land.at[h, s], p_land.at[h, s], p_ss.at[to], p_rs.at[at], device(kc)
            ).wait_recv()
            total = total + p_land[h, s].astype(F32)
        o_rows[h] = total
        for c in range(CHUNKS):
            first = (h * CHUNKS + c) * slim
            out[:, first : first + slim] = o_rows[h, STEPS * c : STEPS * (c + 1), :].astype(BF16)
    for c in range(CHUNKS):
        halve(c).wait_send()
    for h in range(2):
        for kc in range(1, chips):
            reduce(h, kc).wait_send()


def per_device(
    tokens, positions, lengths, w_query, w_key, w_value, w_out, cache_keys, cache_values
):
    n = lax.axis_size("hid")
    width = tokens.shape[2]
    wide = width // CHUNKS
    packed = STEPS * CHUNKS
    query_width, key_width = w_query.shape[1], w_key.shape[1]
    own_heads = query_width // HEAD
    _, capacity, kv_width = cache_keys.shape
    rows = STEPS * n
    message = -(-STEPS * (own_heads + 2) // 16) * 16
    back = -(-STEPS * own_heads // 8) * 8
    smem = pl.BlockSpec(memory_space=pltpu.SMEM)
    vmem = pl.BlockSpec(memory_space=pltpu.VMEM)
    hbm = pl.BlockSpec(memory_space=pltpu.HBM)
    dma = pltpu.SemaphoreType.DMA
    chips = n // 2
    result = pl.pallas_call(
        functools.partial(kernel, n),
        out_shape=pltpu.VMEM((STEPS, width), BF16),
        in_specs=[smem, smem] + [hbm] * 7,
        out_specs=vmem,
        scratch_shapes=[
            pltpu.VMEM((STEPS, width), BF16),
            pltpu.VMEM(w_query.shape, BF16),
            pltpu.VMEM((2 * key_width, width), BF16),
            pltpu.VMEM(w_out.shape, BF16),
            pltpu.VMEM((capacity, kv_width), BF16),
            pltpu.VMEM((capacity, kv_width), BF16),
            pltpu.VMEM((packed, wide), F32),
            pltpu.VMEM((n, packed, wide), BF16),
            pltpu.VMEM((n, packed, wide), F32),
            pltpu.VMEM((CHUNKS, rows, wide), F32),
            pltpu.VMEM((rows, query_width + 2 * HEAD), F32),
            pltpu.VMEM((rows, HEAD), F32),
            pltpu.VMEM((n, message, HEAD), F32),
            pltpu.VMEM((n, message, HEAD), BF16),
            pltpu.VMEM((n, message, HEAD), BF16),
            pltpu.VMEM((n, message, HEAD), F32),
            pltpu.VMEM((STEPS * HEADS, HEAD), F32),
            pltpu.VMEM((STEPS * KV_HEADS, HEAD), F32),
            pltpu.VMEM((STEPS * KV_HEADS, HEAD), F32),
            pltpu.VMEM((n, back, HEAD), F32),
            pltpu.VMEM((n, back, HEAD), F32),
            pltpu.VMEM((rows, query_width), F32),
            pltpu.VMEM((CHUNKS, rows // 2, wide), F32),
            pltpu.VMEM((CHUNKS, rows // 2, wide), BF16),
            pltpu.VMEM((CHUNKS, rows // 2, wide), BF16),
            pltpu.VMEM((2, chips, packed, wide // 2), F32),
            pltpu.VMEM((2, chips, packed, wide // 2), BF16),
            pltpu.VMEM((2, chips, packed, wide // 2), BF16),
            pltpu.VMEM((2, packed, wide // 2), F32),
            dma((7,)),
        ]
        + [dma((n,))] * 6
        + [dma((CHUNKS,))] * 2
        + [dma((2 * chips,))] * 2,
        compiler_params=pltpu.CompilerParams(
            collective_id=0, has_side_effects=True, vmem_limit_bytes=56 * 2**20
        ),
    )(
        positions,
        lengths,
        tokens.reshape(STEPS, width),
        w_query,
        w_key.T,
        w_value.T,
        w_out,
        cache_keys,
        cache_values,
    )
    return result.reshape(tokens.shape)


def solution(mesh):
    return jax.shard_map(
        per_device,
        mesh=mesh,
        in_specs=(
            P(None, ("groups", "hid"), None),
            P(("groups", "hid")),
            P(("groups", "hid")),
            P(None, "hid"),
            P(None, "hid"),
            P(None, "hid"),
            P("hid", None),
            P(("groups", "hid"), None, None),
            P(("groups", "hid"), None, None),
        ),
        out_specs=P(None, ("groups", "hid"), None),
        check_vma=False,
    )
```
